32 devices in a mesh: dp: 4 (over z), tensor: 8 (over y, x, core).
Axes of the slice: x: 2, y: 2, z: 4, core: 2. Of those that a mesh axis runs over, the one named last changes fastest.
Arguments:
- image_rows: bfloat16 [256, 4, 4096], P('tensor', 'dp'), may hold values from -6 to 6
- text_rows: bfloat16 [256, 4, 4096], P('tensor', 'dp'), may hold values from -6 to 6
- text_count: int32 [4], P('dp'), may hold values from 64 to 256, as said below
- slot_kind: int32 [4], replicated, may hold values from 0 to 1, as said below
- attn_gain: float32 [4096], replicated, may hold values from 0.1 to 1.9
- qkv_weight: bfloat16 [4096, 3, 4096], P(None, None, 'tensor'), may hold values from -1 to 1
- out_weight: bfloat16 [4096, 4096], P('tensor'), may hold values from -0.09375 to 0.09375
- expert_gain: float32 [4, 4096], P('dp'), may hold values from 0.1 to 1.9
- expert_in: bfloat16 [4, 4096, 16384], P('dp', None, 'tensor'), may hold values from -0.09375 to 0.09375
- expert_out: bfloat16 [4, 16384, 4096], P('dp', 'tensor'), may hold values from -0.046875 to 0.046875
Outputs:
- image_out: bfloat16 [256, 4, 4096], P('tensor', 'dp')
- text_out: bfloat16 [256, 4, 4096], P('tensor', 'dp')
The draws below stay inside these ranges and needn't reach their ends.
Inputs may be any that keep to these rules, and one draw needn't show every extreme that they name: For each pair the first text_count text slots are live; some pair has 256 and some pair 256 // 4 live text slots. `slot_kind`: exactly 1 of the 4 slots serve one modality (which one is drawn), the rest serve the other, so that one slot receives rows from 4 dp indices.
All inputs are finite; a program needn't handle non-finite values.
Results may differ from the reference program's by a relative error of at most 0.015.
Values may be sent and summed in bfloat16 or wider, within the bound.
A program may use at most 192 MiB of HBM per device.

```python
import math
import jax
import jax.numpy as jnp
from jax import lax

D = 4096
HEADS = 32
HDIM = 128
FF = 16384
SLOT = 256
PAIR_DEV = 1
PAIRS = 4
EXPERTS = 4
MINOR = 1
N_TENSOR = 8


def draw_text_count(key, part):
    counts = jax.random.randint(key, (PAIRS,), SLOT // 4, SLOT + 1).astype(jnp.int32)
    order = jax.random.permutation(jax.random.fold_in(key, 7), PAIRS)
    counts = counts.at[order[0]].set(SLOT)
    counts = counts.at[order[1]].set(SLOT // 4)
    return counts.astype(jnp.int32)


def draw_slot_kind(key, part):
    order = jax.random.permutation(jax.random.fold_in(key, 3), EXPERTS)
    minority = jax.random.randint(jax.random.fold_in(key, 5), (), 0, 2).astype(jnp.int32)
    return jnp.where(order < MINOR, minority, 1 - minority).astype(jnp.int32)


def common_signs(key):
    bits = jax.random.randint(jax.random.fold_in(key, 11), (D,), 0, 2)
    return (2 * bits - 1).astype(jnp.float32)


def row_order(one_key):
    return jax.random.permutation(one_key, SLOT)


def width_order(one_key):
    return jax.random.permutation(one_key, D)


def draw_qkv_weight(key, part):
    scale = (D // 2) ** (-0.5)
    shape = (D, 3, HEADS * HDIM)
    base = jnp.clip(jax.random.normal(jax.random.fold_in(key, 21), shape, jnp.float32), -4.0, 4.0) * scale
    strength = jax.random.uniform(jax.random.fold_in(key, 23), (HEADS,), jnp.float32, 150.0, 300.0)
    per_column = jnp.sqrt(strength / math.sqrt(HDIM)) / D
    per_column = jnp.repeat(per_column, HDIM)
    column_bits = jax.random.randint(jax.random.fold_in(key, 25), (HEADS * HDIM,), 0, 2)
    column_signs = (2 * column_bits - 1).astype(jnp.float32)
    plant = common_signs(key)[:, None] * (per_column * column_signs)[None, :]
    empty = jnp.zeros_like(plant)
    plant = jnp.stack([plant, plant, empty], axis=1)
    return (base + plant).astype(jnp.bfloat16)


def draw_image_rows(key, part):
    shape = (SLOT, PAIRS, D)
    noise = jnp.clip(jax.random.normal(jax.random.fold_in(key, 41), shape, jnp.float32), -6.0, 6.0)
    row_keys = jax.random.split(jax.random.fold_in(key, 31), PAIRS)
    orders = jax.vmap(row_order)(row_keys)
    first = orders[:, 0]
    second = orders[:, 1]
    flip_keys = jax.random.split(jax.random.fold_in(key, 33), PAIRS)
    ranks = jax.vmap(width_order)(flip_keys)
    flip_count = max(1, D // 290)
    flipped = jnp.where(ranks < flip_count, -1.0, 1.0).astype(jnp.float32)
    signs = common_signs(key)
    planted_one = 6.0 * signs[None, None, :]
    planted_two = 6.0 * signs[None, :] * flipped
    row_ids = jnp.arange(SLOT, dtype=jnp.int32)[:, None, None]
    values = jnp.where(row_ids == first[None, :, None], planted_one, noise)
    values = jnp.where(row_ids == second[None, :, None], planted_two[None, :, :], values)
    return values.astype(jnp.bfloat16)


def levels(own_key, extent, shards, low, largest):
    factor_of = 1.0
    for dim, shards_of in shards:
        heights = jax.random.uniform(jax.random.fold_in(jax.random.fold_in(own_key, 6), dim), (shards_of,), jnp.float32, low / len(shards), largest / len(shards))
        factor_of = factor_of * jnp.repeat(jnp.exp(heights), extent[dim] // shards_of).reshape((-1,) + (1,) * (len(extent) - 1 - dim))
    return factor_of


def normal_values(rng, dims, width, bound, cuts=(), kind=jnp.bfloat16):
    drawn = width * jax.random.normal(rng, dims, jnp.float32)
    if cuts:
        drawn = drawn * levels(rng, dims, cuts, -0.22, 0.18)
    return jnp.clip(drawn, -bound, bound).astype(kind)


def setup_inputs(seed: int = 0) -> dict:
    splits = jax.random.split(jax.random.key(seed), 11)
    image_rows = draw_image_rows(jax.random.fold_in(splits[10], 71), 0)
    text_rows = normal_values(splits[1], (SLOT, PAIRS, D), 1.0, 6.0, ((0, 8), (1, 4)))
    text_count = draw_text_count(jax.random.fold_in(splits[10], 71), 0)
    slot_kind = draw_slot_kind(jax.random.fold_in(splits[10], 71), 0)
    attn_gain = jnp.clip(1.0 + 0.18 * jax.random.normal(splits[4], (D,), jnp.float32), 0.1, 1.9)
    qkv_weight = draw_qkv_weight(jax.random.fold_in(splits[10], 71), 0)
    out_weight = normal_values(splits[6], (HEADS * HDIM, D), D ** -0.5, 0.09375, ((0, 8),))
    expert_gain = jnp.clip(1.0 + 0.18 * jax.random.normal(splits[7], (EXPERTS, D), jnp.float32), 0.1, 1.9)
    expert_in = normal_values(splits[8], (EXPERTS, D, FF), D ** -0.5, 0.09375, ((0, 4), (2, 8)))
    expert_out = normal_values(splits[9], (EXPERTS, FF, D), FF ** -0.5, 0.046875, ((0, 4), (1, 8)))
    return dict(image_rows=image_rows, text_rows=text_rows, text_count=text_count, slot_kind=slot_kind, attn_gain=attn_gain, qkv_weight=qkv_weight, out_weight=out_weight, expert_gain=expert_gain, expert_in=expert_in, expert_out=expert_out)


def layer_norm(values, gain):
    floats = values.astype(jnp.float32)
    center = floats - lax.optimization_barrier(jnp.mean(floats, axis=-1, keepdims=True))
    spread = lax.optimization_barrier(jnp.mean(center * center, axis=-1, keepdims=True))
    return center * lax.rsqrt(spread + 1e-05) * gain.astype(jnp.float32)

def route_slot(slot_kind, kind, source):
    member = (slot_kind == kind).astype(jnp.int32)
    member_count = jnp.sum(member)
    member_rank = jnp.cumsum(member) - member
    target = source % member_count
    slot_ids = jnp.arange(slot_kind.shape[0], dtype=jnp.int32)
    picked = jnp.where((member == 1) & (member_rank == target), slot_ids, 0)
    return jnp.sum(picked).astype(jnp.int32)

def reference(image_rows, text_rows, text_count, slot_kind, attn_gain, qkv_weight, out_weight, expert_gain, expert_in, expert_out):
    head_local = HEADS // N_TENSOR
    hidden_local = FF // N_TENSOR
    seq_total = 2 * SLOT
    qkv_flat = qkv_weight.reshape(D, 3 * HEADS * HDIM)
    out_split = out_weight.reshape(N_TENSOR, head_local * HDIM, D).astype(jnp.float32)
    positions = jnp.arange(seq_total, dtype=jnp.int32)

    def attend(pair_id):
        sequence = jnp.concatenate([image_rows[:, pair_id], text_rows[:, pair_id]], axis=0)
        normed = layer_norm(sequence, attn_gain).astype(jnp.bfloat16)
        mixed = jnp.dot(normed, qkv_flat, preferred_element_type=jnp.float32).astype(jnp.bfloat16)
        mixed = mixed.reshape(seq_total, 3, HEADS, HDIM).astype(jnp.float32)
        scores = jnp.einsum('qhk,shk->hqs', mixed[:, 0], mixed[:, 1]) * HDIM ** (-0.5)
        key_live = (positions < SLOT) | (positions - SLOT < text_count[pair_id])
        scores = jnp.where(key_live[None, None, :], scores, -1e+30)
        scores = scores - lax.optimization_barrier(jnp.max(scores, axis=-1, keepdims=True))
        weights = jnp.exp(scores)
        weights = (weights / lax.optimization_barrier(jnp.sum(weights, axis=-1, keepdims=True))).astype(jnp.bfloat16)
        context = jnp.einsum('hqs,shk->qhk', weights.astype(jnp.float32), mixed[:, 2]).astype(jnp.bfloat16)
        context = context.reshape(seq_total, N_TENSOR, head_local * HDIM).astype(jnp.float32)
        partial_sums = jnp.einsum('snk,nkd->nsd', context, out_split).astype(jnp.bfloat16)
        attended = lax.optimization_barrier(jnp.sum(partial_sums.astype(jnp.float32), axis=0))
        return (sequence.astype(jnp.float32) + attended).astype(jnp.bfloat16)
    hidden = lax.map(attend, jnp.arange(PAIRS, dtype=jnp.int32))

    def expert(operands):
        block, slot_id = operands
        normed = layer_norm(block, expert_gain[slot_id]).astype(jnp.bfloat16)
        inner = jnp.dot(normed, expert_in[slot_id], preferred_element_type=jnp.float32)
        inner = jax.nn.gelu(inner, approximate=False).astype(jnp.bfloat16)
        inner = inner.reshape(SLOT, N_TENSOR, hidden_local).astype(jnp.float32)
        down = expert_out[slot_id].reshape(N_TENSOR, hidden_local, D).astype(jnp.float32)
        partial_sums = jnp.einsum('snf,nfd->nsd', inner, down).astype(jnp.bfloat16)
        return lax.optimization_barrier(jnp.sum(partial_sums.astype(jnp.float32), axis=0)).astype(jnp.bfloat16)
    sources = jnp.arange(PAIRS, dtype=jnp.int32) // PAIR_DEV

    def image_slot(source):
        return route_slot(slot_kind, 0, source)

    def text_slot(source):
        return route_slot(slot_kind, 1, source)
    image_slots = jax.vmap(image_slot)(sources)
    text_slots = jax.vmap(text_slot)(sources)
    image_hidden = hidden[:, :SLOT]
    text_hidden = hidden[:, SLOT:]
    image_ffn = lax.map(expert, (image_hidden, image_slots))
    text_ffn = lax.map(expert, (text_hidden, text_slots))
    image_out = (image_hidden.astype(jnp.float32) + image_ffn.astype(jnp.float32)).astype(jnp.bfloat16)
    text_sum = (text_hidden.astype(jnp.float32) + text_ffn.astype(jnp.float32)).astype(jnp.bfloat16)
    live = jnp.arange(SLOT, dtype=jnp.int32)[None, :, None] < text_count[:, None, None]
    text_out = jnp.where(live, text_sum, jnp.zeros_like(text_sum))
    return (jnp.transpose(image_out, (1, 0, 2)), jnp.transpose(text_out, (1, 0, 2)))
```

```python
import functools

import jax
import jax.numpy as jnp
from jax import lax
from jax.experimental import pallas as pl
from jax.experimental.pallas import tpu as pltpu
from jax.sharding import PartitionSpec as P

HDIM = 128
CAP = 4
CHUNKS = 2


def layer_norm(values, gain):
    floats = values.astype(jnp.float32)
    center = floats - jnp.mean(floats, axis=-1, keepdims=True)
    spread = jnp.mean(center * center, axis=-1, keepdims=True)
    return center * lax.rsqrt(spread + 1e-05) * gain


def route_slot(slot_kind, kind, source):
    slot_ids = jnp.arange(slot_kind.shape[0], dtype=jnp.int32)
    member = (slot_kind == kind).astype(jnp.int32)
    member_count = jnp.sum(member)
    earlier = (slot_ids[None, :] < slot_ids[:, None]).astype(jnp.int32)
    member_rank = jnp.sum(earlier * member[None, :], axis=1)
    target = source % member_count
    picked = jnp.where((member == 1) & (member_rank == target), slot_ids, 0)
    return jnp.sum(picked)


def attention_kernel(heads, live_ref, q_ref, k_ref, v_ref, out_ref):
    live = live_ref[...] > 0
    for head in range(heads):
        columns = slice(head * HDIM, (head + 1) * HDIM)
        scores = lax.dot_general(
            q_ref[:, columns],
            k_ref[:, columns],
            (((1,), (1,)), ((), ())),
            preferred_element_type=jnp.float32,
        ) * HDIM ** (-0.5)
        scores = jnp.where(live, scores, -1e30)
        weights = jnp.exp(scores - jnp.max(scores, axis=-1, keepdims=True))
        weights = weights / jnp.sum(weights, axis=-1, keepdims=True)
        out_ref[:, columns] = jnp.dot(
            weights.astype(jnp.bfloat16), v_ref[:, columns], preferred_element_type=jnp.float32
        ).astype(jnp.bfloat16)


def attention(live, queries, keys, values):
    rows, width = queries.shape
    count = keys.shape[0]
    heads = width // HDIM
    return pl.pallas_call(
        functools.partial(attention_kernel, heads),
        out_shape=jax.ShapeDtypeStruct((rows, width), jnp.bfloat16),
        in_specs=[pl.BlockSpec(memory_space=pltpu.VMEM)] * 4,
        out_specs=pl.BlockSpec(memory_space=pltpu.VMEM),
        cost_estimate=pl.CostEstimate(
            flops=4 * rows * count * width,
            bytes_accessed=4 * (rows + count) * width,
            transcendentals=rows * count * heads,
        ),
        compiler_params=pltpu.CompilerParams(vmem_limit_bytes=24 * 2**20),
    )(live, queries, keys, values)


def matmul(left, right):
    return jnp.dot(left, right, preferred_element_type=jnp.float32)


def body(
    image_rows,
    text_rows,
    text_count,
    slot_kind,
    attn_gain,
    qkv_weight,
    out_weight,
    expert_gain,
    expert_in,
    expert_out,
):
    row_count = image_rows.shape[0]
    model_width = image_rows.shape[2]
    tensor_size = lax.axis_size("tensor")
    tensor_place = lax.axis_index("tensor")
    dp_place = lax.axis_index("dp")
    slot_total = slot_kind.shape[0]
    part = row_count // CHUNKS
    stacked = jnp.stack(
        [image_rows.reshape(row_count, model_width), text_rows.reshape(row_count, model_width)]
    )

    def rows_of(chunk):
        return stacked[:, chunk * part : (chunk + 1) * part]

    projected = []
    for chunk in range(CHUNKS):
        normed = layer_norm(rows_of(chunk), attn_gain).astype(jnp.bfloat16)
        gathered = lax.all_gather(normed, "tensor", axis=0).reshape(-1, model_width)
        projected.append(
            [matmul(gathered, qkv_weight[:, i]).astype(jnp.bfloat16) for i in range(3)]
        )
    keys = jnp.concatenate([p[1] for p in projected], axis=0)
    values = jnp.concatenate([p[2] for p in projected], axis=0)
    place = jnp.arange(CHUNKS * tensor_size * 2 * part, dtype=jnp.int32)
    key_chunk, rest = place // (tensor_size * 2 * part), place % (tensor_size * 2 * part)
    key_row = rest // (2 * part) * row_count + key_chunk * part + rest % part
    is_text = rest // part % 2
    live_keys = ((is_text == 0) | (key_row < text_count[0])).astype(jnp.int32)[None, :]

    image_dest = route_slot(slot_kind, 0, dp_place)
    text_dest = route_slot(slot_kind, 1, dp_place)
    slot_ids = jnp.arange(slot_total, dtype=jnp.int32)
    own_kind = lax.dynamic_index_in_dim(slot_kind, dp_place, 0, keepdims=False)
    member = (slot_kind == own_kind).astype(jnp.int32)
    member_count = jnp.sum(member)
    own_rank = jnp.sum(jnp.where(slot_ids < dp_place, member, 0))

    hiddens, arrivals = [], []
    for chunk in range(CHUNKS):
        context = attention(live_keys, projected[chunk][0], keys, values)
        terms = matmul(context, out_weight).astype(jnp.bfloat16)
        terms = terms.reshape(tensor_size, 2 * part, model_width)
        attended = lax.psum_scatter(terms, "tensor", scatter_dimension=0)
        attended = attended.reshape(2, part, model_width).astype(jnp.float32)
        hidden = (rows_of(chunk).astype(jnp.float32) + attended).astype(jnp.bfloat16)
        hiddens.append(hidden)
        outgoing = jnp.where((slot_kind == 0)[:, None, None], hidden[0][None], hidden[1][None])
        arrivals.append(lax.all_to_all(outgoing, "dp", split_axis=0, concat_axis=0, tiled=True))

    images, texts = [], []
    for chunk in range(CHUNKS):
        block = arrivals[chunk]
        if slot_total > CAP:
            senders = [jnp.minimum(own_rank + c * member_count, slot_total - 1) for c in range(CAP)]
            block = jnp.stack([lax.dynamic_index_in_dim(block, s, 0, keepdims=False) for s in senders])
        blocks = block.shape[0]
        scaled = layer_norm(block, expert_gain[0]).astype(jnp.bfloat16)
        gathered = lax.all_gather(scaled, "tensor", axis=0).reshape(-1, model_width)
        inner = jax.nn.gelu(matmul(gathered, expert_in[0]), approximate=False).astype(jnp.bfloat16)
        inner = lax.optimization_barrier(inner)
        terms = matmul(inner, expert_out[0]).astype(jnp.bfloat16)
        terms = terms.reshape(tensor_size, blocks * part, model_width)
        done = lax.psum_scatter(terms, "tensor", scatter_dimension=0)
        done = done.reshape(blocks, part, model_width)
        if slot_total > CAP:
            wanted = [jnp.minimum(d // member_count, CAP - 1) for d in range(slot_total)]
            done = jnp.stack([lax.dynamic_index_in_dim(done, w, 0, keepdims=False) for w in wanted])
        returned = lax.all_to_all(done, "dp", split_axis=0, concat_axis=0, tiled=True)
        image_ffn = lax.dynamic_index_in_dim(returned, image_dest, 0, keepdims=False)
        text_ffn = lax.dynamic_index_in_dim(returned, text_dest, 0, keepdims=False)
        hidden = hiddens[chunk].astype(jnp.float32)
        images.append((hidden[0] + image_ffn.astype(jnp.float32)).astype(jnp.bfloat16))
        text_sum = (hidden[1] + text_ffn.astype(jnp.float32)).astype(jnp.bfloat16)
        slot_index = tensor_place * row_count + chunk * part + jnp.arange(part, dtype=jnp.int32)
        live = slot_index[:, None] < text_count[0]
        texts.append(jnp.where(live, text_sum, jnp.zeros_like(text_sum)))
    shape = image_rows.shape
    return (
        jnp.concatenate(images, axis=0).reshape(shape),
        jnp.concatenate(texts, axis=0).reshape(shape),
    )


def solution(mesh):
    return jax.shard_map(
        body,
        mesh=mesh,
        in_specs=(
            P("tensor", "dp", None),
            P("tensor", "dp", None),
            P("dp"),
            P(),
            P(),
            P(None, None, "tensor"),
            P("tensor", None),
            P("dp", None),
            P("dp", None, "tensor"),
            P("dp", "tensor", None),
        ),
        out_specs=(P("tensor", "dp", None), P("tensor", "dp", None)),
        check_vma=False,
    )
```

```python
import functools

import jax
import jax.numpy as jnp
from jax import lax
from jax.experimental import pallas as pl
from jax.experimental.pallas import tpu as pltpu
from jax.sharding import PartitionSpec as P

HDIM = 128
CAP = 4
CHUNKS = 1
MESH = pl.DeviceIdType.MESH
TILES = 4
PIECES = 4


def layer_norm(values, gain):
    floats = values.astype(jnp.float32)
    center = floats - jnp.mean(floats, axis=-1, keepdims=True)
    spread = jnp.mean(center * center, axis=-1, keepdims=True)
    return center * lax.rsqrt(spread + 1e-05) * gain


def route_slot(slot_kind, kind, source):
    slot_ids = jnp.arange(slot_kind.shape[0], dtype=jnp.int32)
    member = (slot_kind == kind).astype(jnp.int32)
    member_count = jnp.sum(member)
    earlier = (slot_ids[None, :] < slot_ids[:, None]).astype(jnp.int32)
    member_rank = jnp.sum(earlier * member[None, :], axis=1)
    target = source % member_count
    picked = jnp.where((member == 1) & (member_rank == target), slot_ids, 0)
    return jnp.sum(picked)


def attention_kernel(heads, live_ref, q_ref, k_ref, v_ref, out_ref):
    live = live_ref[...] > 0
    for head in range(heads):
        columns = slice(head * HDIM, (head + 1) * HDIM)
        scores = lax.dot_general(
            q_ref[:, columns],
            k_ref[:, columns],
            (((1,), (1,)), ((), ())),
            preferred_element_type=jnp.float32,
        ) * HDIM ** (-0.5)
        scores = jnp.where(live, scores, -1e30)
        weights = jnp.exp(scores - jnp.max(scores, axis=-1, keepdims=True))
        weights = weights / jnp.sum(weights, axis=-1, keepdims=True)
        out_ref[:, columns] = jnp.dot(
            weights.astype(jnp.bfloat16), v_ref[:, columns], preferred_element_type=jnp.float32
        ).astype(jnp.bfloat16)


def attention(live, queries, keys, values):
    rows, width = queries.shape
    count = keys.shape[0]
    heads = width // HDIM
    return pl.pallas_call(
        functools.partial(attention_kernel, heads),
        out_shape=jax.ShapeDtypeStruct((rows, width), jnp.bfloat16),
        in_specs=[pl.BlockSpec(memory_space=pltpu.VMEM)] * 4,
        out_specs=pl.BlockSpec(memory_space=pltpu.VMEM),
        cost_estimate=pl.CostEstimate(
            flops=4 * rows * count * width,
            bytes_accessed=4 * (rows + count) * width,
            transcendentals=rows * count * heads,
        ),
        compiler_params=pltpu.CompilerParams(vmem_limit_bytes=24 * 2**20),
    )(live, queries, keys, values)


def matmul(left, right):
    return jnp.dot(left, right, preferred_element_type=jnp.float32)


def partners():
    me = lax.axis_index("tensor")
    core, across, down = me % 2, me // 2 % 2, me // 4
    sibling = me + 1 - 2 * core
    over_x = me + 2 - 4 * across
    over_y = me + 4 - 8 * down
    return me, core, across, down, sibling, over_x, over_y


def greet(others):
    barrier = pltpu.get_barrier_semaphore()
    for other in others:
        pl.semaphore_signal(barrier, inc=1, device_id={"tensor": other}, device_id_type=MESH)
    pl.semaphore_wait(barrier, len(others))


def remote(source, target, send_sem, recv_sem, other):
    return pltpu.make_async_remote_copy(
        src_ref=source,
        dst_ref=target,
        send_sem=send_sem,
        recv_sem=recv_sem,
        device_id={"tensor": other},
        device_id_type=MESH,
    )


def gather_kernel(own_ref, all_ref, own_sem, send_sem, recv_sem):
    me, core, across, down, sibling, over_x, over_y = partners()
    diagonal = over_x + over_y - me
    rows = own_ref.shape[0]
    size = rows // PIECES
    half = PIECES // 2

    def piece(owner, p):
        return all_ref.at[owner, pl.ds(p * size, size)]

    greet((sibling, over_x, over_y))
    sent = []

    def send(source, owner, p, kind, other):
        copy = remote(source, piece(owner, p), send_sem.at[kind, p], recv_sem.at[kind, p], other)
        copy.start()
        sent.append(copy)

    def arrived(owner, p, kind, other):
        there = piece(owner, p)
        remote(there, there, send_sem.at[kind, p], recv_sem.at[kind, p], other).wait_recv()

    keep = pltpu.make_async_copy(own_ref, all_ref.at[me], own_sem)
    for i in range(PIECES):
        for kind, other, p in ((0, over_x, i), (1, over_y, (i + half) % PIECES)):
            send(own_ref.at[pl.ds(p * size, size)], me, p, kind, other)
    for p in range(PIECES):
        send(own_ref.at[pl.ds(p * size, size)], me, p, 3, sibling)
    keep.start()
    for i in range(PIECES):
        p, q = i, (i + half) % PIECES
        arrived(over_x, p, 0, over_x)
        if p < half:
            send(piece(over_x, p), over_x, p, 2, over_y)
        send(piece(over_x, p), over_x, p, 4, sibling)
        arrived(over_y, q, 1, over_y)
        if q >= half:
            send(piece(over_y, q), over_y, q, 2, over_x)
        send(piece(over_y, q), over_y, q, 5, sibling)
    for i in range(half):
        for p, other in ((i, over_y), (i + half, over_x)):
            arrived(diagonal, p, 2, other)
            send(piece(diagonal, p), diagonal, p, 6, sibling)
    shift = sibling - me
    for kind, owner in ((3, sibling), (4, over_x + shift), (5, over_y + shift), (6, diagonal + shift)):
        for p in range(PIECES):
            arrived(owner, p, kind, sibling)
    for copy in sent:
        copy.wait_send()
    keep.wait()


def gather_rows(values, collective_id):
    size = lax.axis_size("tensor")
    if size != 8:
        return lax.all_gather(values, "tensor", axis=0)
    return pl.pallas_call(
        gather_kernel,
        out_shape=jax.ShapeDtypeStruct((size, *values.shape), values.dtype),
        in_specs=[pl.BlockSpec(memory_space=pl.ANY)],
        out_specs=pl.BlockSpec(memory_space=pl.ANY),
        scratch_shapes=[
            pltpu.SemaphoreType.DMA,
            pltpu.SemaphoreType.DMA((7, PIECES)),
            pltpu.SemaphoreType.DMA((7, PIECES)),
        ],
        compiler_params=pltpu.CompilerParams(collective_id=collective_id, has_side_effects=True),
    )(values)


def scatter_kernel(
    left_ref, weight_ref, out_ref, weight, terms, first, second, third, w_sem, send_sem, recv_sem
):
    me, core, across, down, sibling, over_x, over_y = partners()
    n = left_ref.shape[1]
    half = n // 2
    depth = left_ref.shape[2]
    wide = weight.shape[2]
    step = 512
    loads = [
        pltpu.make_async_copy(
            weight_ref.at[:, pl.ds(j * wide, wide)], weight.at[j], w_sem.at[j]
        )
        for j in range(TILES)
    ]
    for load in loads:
        load.start()
    greet((sibling, over_x, over_y))
    sent = []

    def send(source, target, kind, j, other):
        copy = remote(source, target, send_sem.at[kind, j], recv_sem.at[kind, j], other)
        copy.start()
        sent.append(copy)

    def arrived(there, kind, j, other):
        remote(there, there, send_sem.at[kind, j], recv_sem.at[kind, j], other).wait_recv()

    low, high = pl.ds(0, half), pl.ds(half, half)
    here = 2 * down + across
    beside_x, beside_y = 2 * down + 1 - across, 2 * (1 - down) + across
    opposite = 3 - here

    def add(*refs):
        total = refs[0][...].astype(jnp.float32)
        for ref in refs[1:]:
            total = total + ref[...].astype(jnp.float32)
        return total

    def multiply(j):
        loads[j].wait()

        @pl.loop(0, 4)
        def _(chip):
            rows = left_ref[pl.ds(2 * chip, 2)].reshape(2 * n, depth)
            for c in range(wide // step):
                columns = slice(c * step, (c + 1) * step)
                product = jnp.dot(rows, weight[j, :, columns], preferred_element_type=jnp.float32)
                product = product.astype(terms.dtype).reshape(2, n, step)
                terms[j, 0, chip, :, columns] = product[0]
                terms[j, 1, chip, :, columns] = product[1]

        send(terms.at[j, 1 - core], first.at[j], 0, j, sibling)

    def stage_two(j):
        arrived(first.at[j], 0, j, sibling)

        @pl.loop(0, 4)
        def _(chip):
            first[j, chip] = add(terms.at[j, core, chip], first.at[j, chip]).astype(first.dtype)

        send(first.at[j, opposite, low], second.at[j, 1, low], 1, j, over_x)
        send(first.at[j, opposite, high], second.at[j, 1, high], 2, j, over_y)
        send(first.at[j, beside_x, low], second.at[j, 0, low], 3, j, over_x)
        send(first.at[j, beside_y, high], second.at[j, 0, high], 4, j, over_y)

    def stage_three(j):
        arrived(second.at[j, 1, low], 1, j, over_x)
        arrived(second.at[j, 1, high], 2, j, over_y)
        second[j, 1, low] = add(first.at[j, beside_y, low], second.at[j, 1, low]).astype(second.dtype)
        second[j, 1, high] = add(first.at[j, beside_x, high], second.at[j, 1, high]).astype(second.dtype)
        send(second.at[j, 1, low], third.at[j, low], 5, j, over_y)
        send(second.at[j, 1, high], third.at[j, high], 6, j, over_x)

    def finish(j):
        arrived(second.at[j, 0, low], 3, j, over_x)
        arrived(second.at[j, 0, high], 4, j, over_y)
        arrived(third.at[j, low], 5, j, over_y)
        arrived(third.at[j, high], 6, j, over_x)
        total = add(first.at[j, here], second.at[j, 0], third.at[j])
        out_ref[:, j * wide : (j + 1) * wide] = total.astype(out_ref.dtype)

    for j in range(TILES + 3):
        if j < TILES:
            multiply(j)
        if 1 <= j <= TILES:
            stage_two(j - 1)
        if 2 <= j <= TILES + 1:
            stage_three(j - 2)
        if j >= 3:
            finish(j - 3)
    for copy in sent:
        copy.wait_send()


def multiply_scatter(left, weight, dtype, collective_id):
    size, n, depth = left.shape
    width = weight.shape[1]
    if size != 8:
        terms = matmul(left.reshape(size * n, depth), weight).astype(jnp.bfloat16)
        return lax.psum_scatter(terms.reshape(size, n, width), "tensor", scatter_dimension=0).astype(dtype)
    wide = width // TILES
    return pl.pallas_call(
        scatter_kernel,
        out_shape=jax.ShapeDtypeStruct((n, width), dtype),
        in_specs=[pl.BlockSpec(memory_space=pltpu.VMEM), pl.BlockSpec(memory_space=pl.ANY)],
        out_specs=pl.BlockSpec(memory_space=pltpu.VMEM),
        scratch_shapes=[
            pltpu.VMEM((TILES, depth, wide), jnp.bfloat16),
            pltpu.VMEM((TILES, 2, 4, n, wide), jnp.bfloat16),
            pltpu.VMEM((TILES, 4, n, wide), jnp.bfloat16),
            pltpu.VMEM((TILES, 2, n, wide), jnp.bfloat16),
            pltpu.VMEM((TILES, n, wide), jnp.bfloat16),
            pltpu.SemaphoreType.DMA((TILES,)),
            pltpu.SemaphoreType.DMA((7, TILES)),
            pltpu.SemaphoreType.DMA((7, TILES)),
        ],
        compiler_params=pltpu.CompilerParams(
            collective_id=collective_id, has_side_effects=True, vmem_limit_bytes=52 * 2**20
        ),
        cost_estimate=pl.CostEstimate(
            flops=2 * size * n * depth * width, bytes_accessed=2 * depth * width, transcendentals=0
        ),
    )(left, weight)


def body(
    image_rows,
    text_rows,
    text_count,
    slot_kind,
    attn_gain,
    qkv_weight,
    out_weight,
    expert_gain,
    expert_in,
    expert_out,
):
    row_count = image_rows.shape[0]
    model_width = image_rows.shape[2]
    tensor_size = lax.axis_size("tensor")
    tensor_place = lax.axis_index("tensor")
    dp_place = lax.axis_index("dp")
    slot_total = slot_kind.shape[0]
    part = row_count // CHUNKS
    stacked = jnp.stack(
        [image_rows.reshape(row_count, model_width), text_rows.reshape(row_count, model_width)]
    )

    def rows_of(chunk):
        return stacked[:, chunk * part : (chunk + 1) * part]

    projected = []
    for chunk in range(CHUNKS):
        normed = layer_norm(rows_of(chunk), attn_gain).astype(jnp.bfloat16)
        gathered = gather_rows(normed.reshape(2 * part, model_width), 0).reshape(-1, model_width)
        projected.append(
            [matmul(gathered, qkv_weight[:, i]).astype(jnp.bfloat16) for i in range(3)]
        )
    keys = jnp.concatenate([p[1] for p in projected], axis=0)
    values = jnp.concatenate([p[2] for p in projected], axis=0)
    place = jnp.arange(CHUNKS * tensor_size * 2 * part, dtype=jnp.int32)
    key_chunk, rest = place // (tensor_size * 2 * part), place % (tensor_size * 2 * part)
    key_row = rest // (2 * part) * row_count + key_chunk * part + rest % part
    is_text = rest // part % 2
    live_keys = ((is_text == 0) | (key_row < text_count[0])).astype(jnp.int32)[None, :]

    image_dest = route_slot(slot_kind, 0, dp_place)
    text_dest = route_slot(slot_kind, 1, dp_place)
    slot_ids = jnp.arange(slot_total, dtype=jnp.int32)
    own_kind = lax.dynamic_index_in_dim(slot_kind, dp_place, 0, keepdims=False)
    member = (slot_kind == own_kind).astype(jnp.int32)
    member_count = jnp.sum(member)
    own_rank = jnp.sum(jnp.where(slot_ids < dp_place, member, 0))

    hiddens, arrivals = [], []
    for chunk in range(CHUNKS):
        context = attention(live_keys, projected[chunk][0], keys, values)
        attended = multiply_scatter(
            context.reshape(tensor_size, 2 * part, -1), out_weight, jnp.float32, 2
        )
        attended = attended.reshape(2, part, model_width)
        hidden = (rows_of(chunk).astype(jnp.float32) + attended).astype(jnp.bfloat16)
        hiddens.append(hidden)
        outgoing = jnp.where((slot_kind == 0)[:, None, None], hidden[0][None], hidden[1][None])
        arrivals.append(lax.all_to_all(outgoing, "dp", split_axis=0, concat_axis=0, tiled=True))

    images, texts = [], []
    for chunk in range(CHUNKS):
        block = arrivals[chunk]
        if slot_total > CAP:
            senders = [jnp.minimum(own_rank + c * member_count, slot_total - 1) for c in range(CAP)]
            block = jnp.stack([lax.dynamic_index_in_dim(block, s, 0, keepdims=False) for s in senders])
        blocks = block.shape[0]
        scaled = layer_norm(block, expert_gain[0]).astype(jnp.bfloat16)
        gathered = gather_rows(scaled.reshape(blocks * part, model_width), 1).reshape(-1, model_width)
        inner = jax.nn.gelu(matmul(gathered, expert_in[0]), approximate=False).astype(jnp.bfloat16)
        done = multiply_scatter(
            inner.reshape(tensor_size, blocks * part, -1), expert_out[0], jnp.bfloat16, 3
        )
        done = done.reshape(blocks, part, model_width)
        if slot_total > CAP:
            wanted = [jnp.minimum(d // member_count, CAP - 1) for d in range(slot_total)]
            done = jnp.stack([lax.dynamic_index_in_dim(done, w, 0, keepdims=False) for w in wanted])
        returned = lax.all_to_all(done, "dp", split_axis=0, concat_axis=0, tiled=True)
        image_ffn = lax.dynamic_index_in_dim(returned, image_dest, 0, keepdims=False)
        text_ffn = lax.dynamic_index_in_dim(returned, text_dest, 0, keepdims=False)
        hidden = hiddens[chunk].astype(jnp.float32)
        images.append((hidden[0] + image_ffn.astype(jnp.float32)).astype(jnp.bfloat16))
        text_sum = (hidden[1] + text_ffn.astype(jnp.float32)).astype(jnp.bfloat16)
        slot_index = tensor_place * row_count + chunk * part + jnp.arange(part, dtype=jnp.int32)
        live = slot_index[:, None] < text_count[0]
        texts.append(jnp.where(live, text_sum, jnp.zeros_like(text_sum)))
    shape = image_rows.shape
    return (
        jnp.concatenate(images, axis=0).reshape(shape),
        jnp.concatenate(texts, axis=0).reshape(shape),
    )


def solution(mesh):
    return jax.shard_map(
        body,
        mesh=mesh,
        in_specs=(
            P("tensor", "dp", None),
            P("tensor", "dp", None),
            P("dp"),
            P(),
            P(),
            P(None, None, "tensor"),
            P("tensor", None),
            P("dp", None),
            P("dp", None, "tensor"),
            P("dp", "tensor", None),
        ),
        out_specs=(P("tensor", "dp", None), P("tensor", "dp", None)),
        check_vma=False,
    )
```

```python
import functools

import jax
import jax.numpy as jnp
from jax import lax
from jax.experimental import pallas as pl
from jax.experimental.pallas import tpu as pltpu
from jax.sharding import PartitionSpec as P

HDIM = 128
CAP = 4
CHUNKS = 1
MESH = pl.DeviceIdType.MESH
TILES = 4
PIECES = 4


def layer_norm(values, gain):
    floats = values.astype(jnp.float32)
    center = floats - jnp.mean(floats, axis=-1, keepdims=True)
    spread = jnp.mean(center * center, axis=-1, keepdims=True)
    return center * lax.rsqrt(spread + 1e-05) * gain


def route_slot(slot_kind, kind, source):
    slot_ids = jnp.arange(slot_kind.shape[0], dtype=jnp.int32)
    member = (slot_kind == kind).astype(jnp.int32)
    member_count = jnp.sum(member)
    earlier = (slot_ids[None, :] < slot_ids[:, None]).astype(jnp.int32)
    member_rank = jnp.sum(earlier * member[None, :], axis=1)
    target = source % member_count
    picked = jnp.where((member == 1) & (member_rank == target), slot_ids, 0)
    return jnp.sum(picked)


def attention_kernel(heads, live_ref, q_ref, k_ref, v_ref, out_ref):
    live = live_ref[...] > 0
    for head in range(heads):
        columns = slice(head * HDIM, (head + 1) * HDIM)
        scores = lax.dot_general(
            q_ref[:, columns],
            k_ref[:, columns],
            (((1,), (1,)), ((), ())),
            preferred_element_type=jnp.float32,
        ) * HDIM ** (-0.5)
        scores = jnp.where(live, scores, -1e30)
        weights = jnp.exp(scores - jnp.max(scores, axis=-1, keepdims=True))
        weights = weights / jnp.sum(weights, axis=-1, keepdims=True)
        out_ref[:, columns] = jnp.dot(
            weights.astype(jnp.bfloat16), v_ref[:, columns], preferred_element_type=jnp.float32
        ).astype(jnp.bfloat16)


def attention(live, queries, keys, values):
    rows, width = queries.shape
    count = keys.shape[0]
    heads = width // HDIM
    return pl.pallas_call(
        functools.partial(attention_kernel, heads),
        out_shape=jax.ShapeDtypeStruct((rows, width), jnp.bfloat16),
        in_specs=[pl.BlockSpec(memory_space=pltpu.VMEM)] * 4,
        out_specs=pl.BlockSpec(memory_space=pltpu.VMEM),
        cost_estimate=pl.CostEstimate(
            flops=4 * rows * count * width,
            bytes_accessed=4 * (rows + count) * width,
            transcendentals=rows * count * heads,
        ),
        compiler_params=pltpu.CompilerParams(vmem_limit_bytes=24 * 2**20),
    )(live, queries, keys, values)


def matmul(left, right):
    return jnp.dot(left, right, preferred_element_type=jnp.float32)


def partners():
    me = lax.axis_index("tensor")
    core, across, down = me % 2, me // 2 % 2, me // 4
    sibling = me + 1 - 2 * core
    over_x = me + 2 - 4 * across
    over_y = me + 4 - 8 * down
    return me, core, across, down, sibling, over_x, over_y


def greet(others):
    barrier = pltpu.get_barrier_semaphore()
    for other in others:
        pl.semaphore_signal(barrier, inc=1, device_id={"tensor": other}, device_id_type=MESH)
    pl.semaphore_wait(barrier, len(others))


def remote(source, target, send_sem, recv_sem, other):
    return pltpu.make_async_remote_copy(
        src_ref=source,
        dst_ref=target,
        send_sem=send_sem,
        recv_sem=recv_sem,
        device_id={"tensor": other},
        device_id_type=MESH,
    )


def gather_kernel(
    gelu, own_ref, weight_ref, out_ref, weight, all_ref, own_sem, w_sem, send_sem, recv_sem
):
    me, core, across, down, sibling, over_x, over_y = partners()
    diagonal = over_x + over_y - me
    shift = sibling - me
    rows = own_ref.shape[0]
    size = rows // PIECES
    half = PIECES // 2
    tiles, _, wide = weight.shape
    per = weight_ref.shape[2] // wide
    loads = [
        pltpu.make_async_copy(
            weight_ref.at[j // per, :, pl.ds(j % per * wide, wide)], weight.at[j], w_sem.at[j]
        )
        for j in range(tiles)
    ]
    for load in loads:
        load.start()
    keep = pltpu.make_async_copy(own_ref, all_ref.at[me], own_sem)
    keep.start()

    def piece(owner, p):
        return all_ref.at[owner, pl.ds(p * size, size)]

    greet((sibling, over_x, over_y))
    sent = []

    def send(source, owner, p, kind, other):
        copy = remote(source, piece(owner, p), send_sem.at[kind, p], recv_sem.at[kind, p], other)
        copy.start()
        sent.append(copy)

    def arrived(owner, p, kind, other):
        there = piece(owner, p)
        remote(there, there, send_sem.at[kind, p], recv_sem.at[kind, p], other).wait_recv()

    def multiply(blocks):
        @pl.loop(0, tiles)
        def _(j):
            left = jnp.concatenate([all_ref[o, pl.ds(r, c)] for o, r, c in blocks], axis=0)
            product = jnp.dot(left, weight[j], preferred_element_type=jnp.float32)
            if gelu:
                product = 0.5 * product * (1.0 + lax.erf(product * 0.5**0.5))
            product = product.astype(out_ref.dtype)
            columns = pl.ds(pl.multiple_of(j * wide, wide), wide)
            start = 0
            for o, r, c in blocks:
                out_ref[o, pl.ds(r, c), columns] = product[start : start + c]
                start += c

    for i in range(PIECES):
        for kind, other, p in ((0, over_x, i), (1, over_y, (i + half) % PIECES)):
            send(own_ref.at[pl.ds(p * size, size)], me, p, kind, other)
    for p in range(PIECES):
        send(own_ref.at[pl.ds(p * size, size)], me, p, 3, sibling)
    for load in loads:
        load.wait()
    keep.wait()
    for p in range(PIECES):
        arrived(sibling, p, 3, sibling)
    multiply([(me, 0, rows), (sibling, 0, rows)])

    def pass_on(i):
        p, q = i, (i + half) % PIECES
        arrived(over_x, p, 0, over_x)
        if p < half:
            send(piece(over_x, p), over_x, p, 2, over_y)
        arrived(over_y, q, 1, over_y)
        if q >= half:
            send(piece(over_y, q), over_y, q, 2, over_x)
        send(piece(over_x, p), over_x, p, 4, sibling)
        send(piece(over_y, q), over_y, q, 5, sibling)

    def neighbours(first):
        for i in range(first, first + half):
            arrived(over_x + shift, i, 4, sibling)
            arrived(over_y + shift, (i + half) % PIECES, 5, sibling)
        low, high = first * size, (first + half) % PIECES * size
        multiply(
            [(o, r, half * size) for o, r in (
                (over_x, low), (over_x + shift, low), (over_y, high), (over_y + shift, high)
            )]
        )

    for i in range(half):
        pass_on(i)
    neighbours(0)
    for i in range(half, PIECES):
        pass_on(i)
    neighbours(half)
    for i in range(half):
        for p, other in ((i, over_y), (i + half, over_x)):
            arrived(diagonal, p, 2, other)
            send(piece(diagonal, p), diagonal, p, 6, sibling)
    for p in range(PIECES):
        arrived(diagonal + shift, p, 6, sibling)
    multiply([(diagonal, 0, rows), (diagonal + shift, 0, rows)])
    for copy in sent:
        copy.wait_send()


def gather_multiply(values, weight, gelu, collective_id):
    size = lax.axis_size("tensor")
    n, depth = values.shape
    width = weight.shape[0] * weight.shape[2]
    if size != 8:
        gathered = lax.all_gather(values, "tensor", axis=0).reshape(size * n, depth)
        product = jnp.concatenate([matmul(gathered, w) for w in weight], axis=1)
        if gelu:
            product = jax.nn.gelu(product, approximate=False)
        return product.astype(jnp.bfloat16).reshape(size, n, width)
    wide = 256
    return pl.pallas_call(
        functools.partial(gather_kernel, gelu),
        out_shape=jax.ShapeDtypeStruct((size, n, width), values.dtype),
        in_specs=[pl.BlockSpec(memory_space=pltpu.VMEM), pl.BlockSpec(memory_space=pl.ANY)],
        out_specs=pl.BlockSpec(memory_space=pltpu.VMEM),
        scratch_shapes=[
            pltpu.VMEM((width // wide, depth, wide), jnp.bfloat16),
            pltpu.VMEM((size, n, depth), jnp.bfloat16),
            pltpu.SemaphoreType.DMA,
            pltpu.SemaphoreType.DMA((width // wide,)),
            pltpu.SemaphoreType.DMA((7, PIECES)),
            pltpu.SemaphoreType.DMA((7, PIECES)),
        ],
        compiler_params=pltpu.CompilerParams(
            collective_id=collective_id, has_side_effects=True, vmem_limit_bytes=52 * 2**20
        ),
        cost_estimate=pl.CostEstimate(
            flops=2 * size * n * depth * width, bytes_accessed=2 * depth * width, transcendentals=0
        ),
    )(values, weight)


def scatter_kernel(
    left_ref, weight_ref, out_ref, weight, terms, first, second, third, w_sem, send_sem, recv_sem
):
    me, core, across, down, sibling, over_x, over_y = partners()
    n = left_ref.shape[1]
    half = n // 2
    depth = left_ref.shape[2]
    wide = weight.shape[2]
    step = 512
    loads = [
        pltpu.make_async_copy(
            weight_ref.at[:, pl.ds(j * wide, wide)], weight.at[j], w_sem.at[j]
        )
        for j in range(TILES)
    ]
    for load in loads:
        load.start()
    greet((sibling, over_x, over_y))
    sent = []

    def send(source, target, kind, j, other):
        copy = remote(source, target, send_sem.at[kind, j], recv_sem.at[kind, j], other)
        copy.start()
        sent.append(copy)

    def arrived(there, kind, j, other):
        remote(there, there, send_sem.at[kind, j], recv_sem.at[kind, j], other).wait_recv()

    low, high = pl.ds(0, half), pl.ds(half, half)
    here = 2 * down + across
    beside_x, beside_y = 2 * down + 1 - across, 2 * (1 - down) + across
    opposite = 3 - here

    def add(*refs):
        total = refs[0][...].astype(jnp.float32)
        for ref in refs[1:]:
            total = total + ref[...].astype(jnp.float32)
        return total

    def multiply(j):
        loads[j].wait()

        @pl.loop(0, 4)
        def _(chip):
            rows = left_ref[pl.ds(2 * chip, 2)].reshape(2 * n, depth)
            for c in range(wide // step):
                columns = slice(c * step, (c + 1) * step)
                product = jnp.dot(rows, weight[j, :, columns], preferred_element_type=jnp.float32)
                product = product.astype(terms.dtype).reshape(2, n, step)
                terms[j, 0, chip, :, columns] = product[0]
                terms[j, 1, chip, :, columns] = product[1]

        send(terms.at[j, 1 - core], first.at[j], 0, j, sibling)

    def stage_two(j):
        arrived(first.at[j], 0, j, sibling)

        @pl.loop(0, 4)
        def _(chip):
            first[j, chip] = add(terms.at[j, core, chip], first.at[j, chip]).astype(first.dtype)

        send(first.at[j, opposite, low], second.at[j, 1, low], 1, j, over_x)
        send(first.at[j, opposite, high], second.at[j, 1, high], 2, j, over_y)
        send(first.at[j, beside_x, low], second.at[j, 0, low], 3, j, over_x)
        send(first.at[j, beside_y, high], second.at[j, 0, high], 4, j, over_y)

    def stage_three(j):
        arrived(second.at[j, 1, low], 1, j, over_x)
        arrived(second.at[j, 1, high], 2, j, over_y)
        second[j, 1, low] = add(first.at[j, beside_y, low], second.at[j, 1, low]).astype(second.dtype)
        second[j, 1, high] = add(first.at[j, beside_x, high], second.at[j, 1, high]).astype(second.dtype)
        send(second.at[j, 1, low], third.at[j, low], 5, j, over_y)
        send(second.at[j, 1, high], third.at[j, high], 6, j, over_x)

    def finish(j):
        arrived(second.at[j, 0, low], 3, j, over_x)
        arrived(second.at[j, 0, high], 4, j, over_y)
        arrived(third.at[j, low], 5, j, over_y)
        arrived(third.at[j, high], 6, j, over_x)
        total = add(first.at[j, here], second.at[j, 0], third.at[j])
        out_ref[:, j * wide : (j + 1) * wide] = total.astype(out_ref.dtype)

    for j in range(TILES + 3):
        if j < TILES:
            multiply(j)
        if 1 <= j <= TILES:
            stage_two(j - 1)
        if 2 <= j <= TILES + 1:
            stage_three(j - 2)
        if j >= 3:
            finish(j - 3)
    for copy in sent:
        copy.wait_send()


def multiply_scatter(left, weight, dtype, collective_id):
    size, n, depth = left.shape
    width = weight.shape[1]
    if size != 8:
        terms = matmul(left.reshape(size * n, depth), weight).astype(jnp.bfloat16)
        return lax.psum_scatter(terms.reshape(size, n, width), "tensor", scatter_dimension=0).astype(dtype)
    wide = width // TILES
    return pl.pallas_call(
        scatter_kernel,
        out_shape=jax.ShapeDtypeStruct((n, width), dtype),
        in_specs=[pl.BlockSpec(memory_space=pltpu.VMEM), pl.BlockSpec(memory_space=pl.ANY)],
        out_specs=pl.BlockSpec(memory_space=pltpu.VMEM),
        scratch_shapes=[
            pltpu.VMEM((TILES, depth, wide), jnp.bfloat16),
            pltpu.VMEM((TILES, 2, 4, n, wide), jnp.bfloat16),
            pltpu.VMEM((TILES, 4, n, wide), jnp.bfloat16),
            pltpu.VMEM((TILES, 2, n, wide), jnp.bfloat16),
            pltpu.VMEM((TILES, n, wide), jnp.bfloat16),
            pltpu.SemaphoreType.DMA((TILES,)),
            pltpu.SemaphoreType.DMA((7, TILES)),
            pltpu.SemaphoreType.DMA((7, TILES)),
        ],
        compiler_params=pltpu.CompilerParams(
            collective_id=collective_id, has_side_effects=True, vmem_limit_bytes=52 * 2**20
        ),
        cost_estimate=pl.CostEstimate(
            flops=2 * size * n * depth * width, bytes_accessed=2 * depth * width, transcendentals=0
        ),
    )(left, weight)


def body(
    image_rows,
    text_rows,
    text_count,
    slot_kind,
    attn_gain,
    qkv_weight,
    out_weight,
    expert_gain,
    expert_in,
    expert_out,
):
    row_count = image_rows.shape[0]
    model_width = image_rows.shape[2]
    tensor_size = lax.axis_size("tensor")
    tensor_place = lax.axis_index("tensor")
    dp_place = lax.axis_index("dp")
    slot_total = slot_kind.shape[0]
    part = row_count // CHUNKS
    stacked = jnp.stack(
        [image_rows.reshape(row_count, model_width), text_rows.reshape(row_count, model_width)]
    )

    def rows_of(chunk):
        return stacked[:, chunk * part : (chunk + 1) * part]

    projected = []
    for chunk in range(CHUNKS):
        normed = layer_norm(rows_of(chunk), attn_gain).astype(jnp.bfloat16)
        mixed = gather_multiply(
            normed.reshape(2 * part, model_width), jnp.transpose(qkv_weight, (1, 0, 2)), False, 0
        )
        projected.append(jnp.split(mixed.reshape(tensor_size * 2 * part, -1), 3, axis=1))
    keys = jnp.concatenate([p[1] for p in projected], axis=0)
    values = jnp.concatenate([p[2] for p in projected], axis=0)
    place = jnp.arange(CHUNKS * tensor_size * 2 * part, dtype=jnp.int32)
    key_chunk, rest = place // (tensor_size * 2 * part), place % (tensor_size * 2 * part)
    key_row = rest // (2 * part) * row_count + key_chunk * part + rest % part
    is_text = rest // part % 2
    live_keys = ((is_text == 0) | (key_row < text_count[0])).astype(jnp.int32)[None, :]

    image_dest = route_slot(slot_kind, 0, dp_place)
    text_dest = route_slot(slot_kind, 1, dp_place)
    slot_ids = jnp.arange(slot_total, dtype=jnp.int32)
    own_kind = lax.dynamic_index_in_dim(slot_kind, dp_place, 0, keepdims=False)
    member = (slot_kind == own_kind).astype(jnp.int32)
    member_count = jnp.sum(member)
    own_rank = jnp.sum(jnp.where(slot_ids < dp_place, member, 0))

    hiddens, arrivals = [], []
    for chunk in range(CHUNKS):
        context = attention(live_keys, projected[chunk][0], keys, values)
        attended = multiply_scatter(
            context.reshape(tensor_size, 2 * part, -1), out_weight, jnp.float32, 2
        )
        attended = attended.reshape(2, part, model_width)
        hidden = (rows_of(chunk).astype(jnp.float32) + attended).astype(jnp.bfloat16)
        hiddens.append(hidden)
        outgoing = jnp.where((slot_kind == 0)[:, None, None], hidden[0][None], hidden[1][None])
        arrivals.append(lax.all_to_all(outgoing, "dp", split_axis=0, concat_axis=0, tiled=True))

    images, texts = [], []
    for chunk in range(CHUNKS):
        block = arrivals[chunk]
        if slot_total > CAP:
            senders = [jnp.minimum(own_rank + c * member_count, slot_total - 1) for c in range(CAP)]
            block = jnp.stack([lax.dynamic_index_in_dim(block, s, 0, keepdims=False) for s in senders])
        blocks = block.shape[0]
        scaled = layer_norm(block, expert_gain[0]).astype(jnp.bfloat16)
        inner = gather_multiply(
            scaled.reshape(blocks * part, model_width), expert_in, True, 1
        )
        done = multiply_scatter(
            inner, expert_out[0], jnp.bfloat16, 3
        )
        done = done.reshape(blocks, part, model_width)
        if slot_total > CAP:
            wanted = [jnp.minimum(d // member_count, CAP - 1) for d in range(slot_total)]
            done = jnp.stack([lax.dynamic_index_in_dim(done, w, 0, keepdims=False) for w in wanted])
        returned = lax.all_to_all(done, "dp", split_axis=0, concat_axis=0, tiled=True)
        image_ffn = lax.dynamic_index_in_dim(returned, image_dest, 0, keepdims=False)
        text_ffn = lax.dynamic_index_in_dim(returned, text_dest, 0, keepdims=False)
        hidden = hiddens[chunk].astype(jnp.float32)
        images.append((hidden[0] + image_ffn.astype(jnp.float32)).astype(jnp.bfloat16))
        text_sum = (hidden[1] + text_ffn.astype(jnp.float32)).astype(jnp.bfloat16)
        slot_index = tensor_place * row_count + chunk * part + jnp.arange(part, dtype=jnp.int32)
        live = slot_index[:, None] < text_count[0]
        texts.append(jnp.where(live, text_sum, jnp.zeros_like(text_sum)))
    shape = image_rows.shape
    return (
        jnp.concatenate(images, axis=0).reshape(shape),
        jnp.concatenate(texts, axis=0).reshape(shape),
    )


def solution(mesh):
    return jax.shard_map(
        body,
        mesh=mesh,
        in_specs=(
            P("tensor", "dp", None),
            P("tensor", "dp", None),
            P("dp"),
            P(),
            P(),
            P(None, None, "tensor"),
            P("tensor", None),
            P("dp", None),
            P("dp", None, "tensor"),
            P("dp", "tensor", None),
        ),
        out_specs=(P("tensor", "dp", None), P("tensor", "dp", None)),
        check_vma=False,
    )
```
